512 devices in a mesh: fsdp: 32 (over z, x_lo), tensor: 16 (over y, x_hi, core).
Axes of the slice: x: 4 (x_hi: 2, x_lo: 2; x = x_hi * 2 + x_lo), y: 4, z: 16, core: 2. Of those that a mesh axis runs over, the one named last changes fastest.
Arguments:
- tokens: bfloat16 [65536, 3072], P(('fsdp', 'tensor')), may hold values from -6 to 6
- positions: int32 [65536], P(('fsdp', 'tensor')), may hold values from 0 to 4095
- key_weight: bfloat16 [3072, 48, 128], P('fsdp', 'tensor'), may hold values from -0.109375 to 0.109375
- key_bias: bfloat16 [48, 128], P('tensor'), may hold values from -3 to 3
- conv_taps: float32 [48, 3, 128], P('tensor'), may hold values from -3 to 3
Outputs:
- keys_out: bfloat16 [65536, 48, 128], P('fsdp', 'tensor')
The draws below stay inside these ranges and needn't reach their ends.
All inputs are finite; a program needn't handle non-finite values.
Results may differ from the reference program's by a relative error of at most 0.001.
Values may be sent and summed in bfloat16 or wider, within the bound.
No kernel may reach another device: no remote copies, remote signals or barrier semaphores. Data moves between devices by JAX's collectives and lax.ppermute only.
A program may use at most 64 MiB of HBM per device.

```python
import jax
import jax.numpy as jnp
from jax import lax

D = 3072
HEADS = 48
HEAD_DIM = 128
SEQ_LEN = 1024
TOKENS = 65536


def with_ends(values, rng, least, largest):
    longest = values.shape.index(max(values.shape))
    spots = []
    for shift in (0, 1):
        where = [jax.random.randint(jax.random.fold_in(rng, axis), (), 0, length) for axis, length in enumerate(values.shape)]
        where[longest] = (where[longest] + shift) % values.shape[longest]
        spots.append(tuple(where))
    return values.at[spots[0]].set(least).at[spots[1]].set(largest)


def steps_of(own_key, extent, pieces, smallest, largest):
    level, own = 1.0, jax.random.fold_in(own_key, 6)
    for dim, blocks in pieces:
        steps = jnp.exp(jax.random.uniform(jax.random.fold_in(own, dim), (blocks,), jnp.float32, smallest / len(pieces), largest / len(pieces)))
        level = level * jnp.repeat(steps, extent[dim] // blocks).reshape([-1 if axis == dim else 1 for axis in range(len(extent))])
    return level


def centred(stream_key, extent, width, limit, shards=(), kind=jnp.bfloat16):
    factor_of = steps_of(stream_key, extent, shards, -0.22, 0.18) if shards else 1.0
    entries = jax.random.normal(stream_key, extent, jnp.float32) * width * factor_of
    return jnp.minimum(jnp.maximum(entries, -limit), limit).astype(kind)


def setup_inputs(seed: int = 0) -> dict:
    arg_keys = jax.random.split(jax.random.key(seed), 6)
    tokens = centred(arg_keys[0], (TOKENS, D), 1.0, 6.0, ((0, 512),))
    positions = with_ends(jax.random.randint(arg_keys[1], (TOKENS,), 0, 4096), jax.random.fold_in(arg_keys[1], 1), 0, 4095).astype(jnp.int32)
    key_weight = centred(arg_keys[2], (D, HEADS, HEAD_DIM), D ** -0.5, 0.109375, ((0, 32), (1, 16)))
    key_bias = centred(arg_keys[3], (HEADS, HEAD_DIM), 0.5, 3.0, ((0, 16),))
    conv_taps = centred(arg_keys[4], (HEADS, 3, HEAD_DIM), 0.6, 3.0, ((0, 16),), jnp.float32)
    return {"tokens": tokens, "positions": positions, "key_weight": key_weight, "key_bias": key_bias, "conv_taps": conv_taps}


rope_base = 10000.0


def finish(projected, places, key_bias, conv_taps, seq_len):
    row_count = projected.shape[0]
    head_count = key_bias.shape[0]
    projected = projected.reshape(row_count // seq_len, seq_len, head_count, HEAD_DIM) + key_bias.astype(jnp.float32)[None, None]
    zero_row = jnp.zeros((row_count // seq_len, 1, head_count, HEAD_DIM), jnp.float32)
    previous_one = jnp.concatenate([zero_row, projected[:, :-1]], axis=1)
    previous_two = jnp.concatenate([zero_row, previous_one[:, :-1]], axis=1)
    taps_f = conv_taps.astype(jnp.float32)
    convolved = taps_f[None, None, :, 0] * projected + taps_f[None, None, :, 1] * previous_one + taps_f[None, None, :, 2] * previous_two
    convolved = convolved.reshape(row_count, head_count, HEAD_DIM)
    half_dim = HEAD_DIM // 2
    inv_freq = rope_base ** (-(jnp.arange(half_dim, dtype=jnp.float32) * 2.0) / HEAD_DIM)
    angles = places.astype(jnp.float32)[:, None] * inv_freq[None, :]
    cosine = jnp.cos(angles)[:, None, :]
    sine = jnp.sin(angles)[:, None, :]
    first_half = convolved[..., :half_dim]
    second_half = convolved[..., half_dim:]
    new_first = first_half * cosine - second_half * sine
    new_second = second_half * cosine + first_half * sine
    result = jnp.concatenate([new_first, new_second], axis=-1)
    return result.astype(jnp.bfloat16)


def reference(tokens, positions, key_weight, key_bias, conv_taps):
    flat_weight = key_weight.reshape(D, HEADS * HEAD_DIM)
    sequences = tokens.reshape(TOKENS // SEQ_LEN, SEQ_LEN, D)
    seq_places = positions.reshape(TOKENS // SEQ_LEN, SEQ_LEN)

    def per_sequence(pair_args):
        seq_tokens, seq_pos = pair_args
        projected = jnp.dot(seq_tokens, flat_weight, preferred_element_type=jnp.float32)
        return finish(projected, seq_pos, key_bias, conv_taps, SEQ_LEN)

    output = lax.map(per_sequence, (sequences, seq_places))
    return output.reshape(TOKENS, HEADS, HEAD_DIM)
```

```python
import jax
import jax.numpy as jnp
from jax import lax
from jax.experimental import pallas as pl
from jax.experimental.pallas import tpu as pltpu
from jax.sharding import PartitionSpec as P

HEAD_DIM = 128
SEQ_LEN = 1024
rope_base = 10000.0

Y, X_HI, CORE = 4, 2, 2
BATCH = 4


def keys_kernel(shards, rows, place_ref, *refs):
    token_refs = refs[:shards]
    w_ref, bias_ref, taps_ref, cos_ref, sin_ref, out_ref, held, w_flat, proj, sems = refs[shards:]
    copies = [pltpu.make_async_copy(token_refs[i], held.at[i], sems.at[i]) for i in range(shards)]
    for copy in copies:
        copy.start()
    heads = out_ref.shape[0]
    piece_rows = w_ref.shape[1] // heads
    for piece in range(w_ref.shape[0]):
        for head in range(heads):
            w_flat[piece * piece_rows : (piece + 1) * piece_rows, head * HEAD_DIM : (head + 1) * HEAD_DIM] = w_ref[
                piece, head * piece_rows : (head + 1) * piece_rows, :
            ]
    proj[0:8, :] = jnp.zeros((8, proj.shape[1]), jnp.float32)
    for first in range(0, shards, BATCH):
        for copy in copies[first : first + BATCH]:
            copy.wait()
        block = held[first : first + BATCH].reshape(BATCH * rows, held.shape[2])
        raw = jnp.dot(block, w_flat[...], preferred_element_type=jnp.float32) + bias_ref[...]
        for i in range(BATCH):
            start = pl.multiple_of(place_ref[first + i] * rows + 8, 8)
            proj[pl.ds(start, rows), :] = raw[i * rows : (i + 1) * rows]

    @pl.loop(0, shards)
    def _(shard):
        start = pl.multiple_of(shard * rows, rows)
        tail = proj[pl.ds(start, 8), :]
        tail = jnp.where(lax.rem(shard, SEQ_LEN // rows) == 0, 0.0, tail)
        cosine = cos_ref[pl.ds(start, rows), :]
        sine = sin_ref[pl.ds(start, rows), :]
        row = lax.broadcasted_iota(jnp.int32, (rows, HEAD_DIM), 0)
        for head in range(heads):
            lanes = slice(head * HEAD_DIM, (head + 1) * HEAD_DIM)
            now = proj[pl.ds(start + 8, rows), lanes]
            before_one, before_two = tail[7:8, lanes], tail[6:7, lanes]
            previous_one = jnp.where(row == 0, before_one, pltpu.roll(now, 1, 0))
            previous_two = jnp.where(row == 0, before_two, jnp.where(row == 1, before_one, pltpu.roll(now, 2, 0)))
            part = taps_ref[0:1, lanes] * now + taps_ref[1:2, lanes] * previous_one + taps_ref[2:3, lanes] * previous_two
            turned = part * cosine + pltpu.roll(part, HEAD_DIM // 2, 1) * sine
            out_ref[head, pl.ds(start, rows), :] = turned.astype(out_ref.dtype)


def rotation(places):
    half_dim = HEAD_DIM // 2
    inv_freq = rope_base ** (-(jnp.arange(half_dim, dtype=jnp.float32) * 2.0) / HEAD_DIM)
    angles = places.astype(jnp.float32)[:, None] * inv_freq[None, :]
    cosine = jnp.cos(angles)
    sine = jnp.sin(angles)
    return jnp.concatenate([cosine, cosine], axis=1), jnp.concatenate([-sine, sine], axis=1)


def shifted(y_step, x_step, core_step):
    pairs = []
    for y in range(Y):
        for x in range(X_HI):
            for c in range(CORE):
                there = (((y + y_step) % Y) * X_HI + (x + x_step) % X_HI) * CORE + (c + core_step) % CORE
                pairs.append(((y * X_HI + x) * CORE + c, there))
    return pairs


def body(fsdp, tensor, tokens, positions, key_weight, key_bias, conv_taps):
    rows, depth = tokens.shape
    piece, heads, _ = key_weight.shape
    columns = heads * HEAD_DIM

    own_weight = jnp.transpose(key_weight, (1, 0, 2))
    near_weight = lax.ppermute(own_weight, "fsdp", [(i, i ^ 1) for i in range(fsdp)])
    is_low = lax.axis_index("fsdp") % 2 == 0
    first = jnp.where(is_low, own_weight, near_weight)
    second = jnp.where(is_low, near_weight, own_weight)
    pair = jnp.concatenate([first, second], axis=1).reshape(heads * 2 * piece, HEAD_DIM)
    line_groups = [[2 * i + j for i in range(fsdp // 2)] for j in range(2)]
    weight = lax.all_gather(pair, "fsdp", axis=0, axis_index_groups=line_groups)

    tokens, positions, pair = lax.optimization_barrier((tokens, positions, pair))
    me = lax.axis_index("tensor")
    my_y, my_x, my_core = me // (X_HI * CORE), me // CORE % X_HI, me % CORE
    blocks, places_of = [], []
    for x_step in range(X_HI):
        for y_step in (0, 1, 3, 2):
            block = tokens if x_step == 0 and y_step == 0 else lax.ppermute(tokens, "tensor", shifted(y_step, x_step, 0))
            blocks.append(block)
            places_of.append(((my_y + Y - y_step) % Y) * X_HI + (my_x + x_step) % X_HI)
    across = [lax.ppermute(block, "tensor", shifted(0, 0, 1)) for block in blocks]
    place = jnp.stack([p * CORE + my_core for p in places_of] + [p * CORE + 1 - my_core for p in places_of])

    places = lax.all_gather(positions, "tensor", axis=0, tiled=True)
    cosine, sine = rotation(places)

    taps = jnp.transpose(conv_taps, (1, 0, 2)).reshape(conv_taps.shape[1], columns)
    bias = key_bias.astype(jnp.float32).reshape(1, columns)
    total = rows * tensor
    vmem = pl.BlockSpec(memory_space=pltpu.VMEM)
    keys = pl.pallas_call(
        lambda *refs: keys_kernel(tensor, rows, *refs),
        in_specs=[pl.BlockSpec(memory_space=pltpu.SMEM)] + [pl.BlockSpec(memory_space=pl.ANY)] * tensor + [vmem] * 5,
        out_specs=vmem,
        out_shape=jax.ShapeDtypeStruct((heads, total, HEAD_DIM), jnp.bfloat16),
        scratch_shapes=[
            pltpu.VMEM((tensor, rows, depth), jnp.bfloat16),
            pltpu.VMEM((depth, columns), jnp.bfloat16),
            pltpu.VMEM((total + 8, columns), jnp.float32),
            pltpu.SemaphoreType.DMA((tensor,)),
        ],
        compiler_params=pltpu.CompilerParams(vmem_limit_bytes=56 * 1024 * 1024),
        cost_estimate=pl.CostEstimate(
            flops=2 * total * depth * columns,
            bytes_accessed=2 * (total * depth + depth * columns + total * columns),
            transcendentals=0,
        ),
    )(place, *blocks, *across, weight, bias, taps, cosine, sine)
    return jnp.transpose(keys, (1, 0, 2))


def solution(mesh):
    fsdp, tensor = mesh.shape["fsdp"], mesh.shape["tensor"]
    return jax.shard_map(
        lambda *args: body(fsdp, tensor, *args),
        mesh=mesh,
        in_specs=(
            P(("fsdp", "tensor"), None),
            P(("fsdp", "tensor")),
            P("fsdp", "tensor", None),
            P("tensor", None),
            P("tensor", None, None),
        ),
        out_specs=P("fsdp", "tensor", None),
        check_vma=False,
    )
```

```python
import jax
import jax.numpy as jnp
from jax import lax
from jax.experimental import pallas as pl
from jax.experimental.pallas import tpu as pltpu
from jax.sharding import Mesh
from jax.sharding import PartitionSpec as P

HEAD_DIM = 128
SEQ_LEN = 1024
rope_base = 10000.0

Y, X_HI, CORE = 4, 2, 2
BATCH = 4
NEAR = 64


def keys_kernel(where_ref, *refs):
    count = Y + 2
    (*near_own, far_own_ref, far_other_ref), (*near_across, x_far_own_ref, x_far_other_ref) = refs[:count], refs[count : 2 * count]
    refs = refs[2 * count :]
    w_ref, bias_ref, taps_ref, turns_ref, out_ref, held, w_flat, turns, keys, turns_sem, out_sems, w_sems, sems = refs
    shards, rows, depth = held.shape
    pieces, heads = w_ref.shape[0], out_ref.shape[0]
    piece_rows = w_ref.shape[1] // heads
    my_x, my_core, my_y = where_ref[0], where_ref[1], where_ref[2]
    loads = []
    for piece in range(pieces):
        for head in range(heads):
            loads.append(
                pltpu.make_async_copy(
                    w_ref.at[piece, pl.ds(head * piece_rows, piece_rows), :],
                    w_flat.at[pl.ds(piece * piece_rows, piece_rows), pl.ds(head * HEAD_DIM, HEAD_DIM)],
                    w_sems.at[piece * heads + head],
                )
            )
    per_block = BATCH // (X_HI * CORE)

    def copies_of(y, source_y, kept):
        copies = []
        for x_step in range(X_HI):
            chip = y * X_HI + jnp.bitwise_xor(my_x, x_step)
            for core_step, near, far in (
                (0, near_own[kept], (far_own_ref, far_other_ref)[x_step]),
                (1, near_across[kept], (x_far_own_ref, x_far_other_ref)[x_step]),
            ):
                shard = chip * CORE + jnp.bitwise_xor(my_core, core_step)
                for source, start, size in ((near.at[x_step], 0, NEAR), (far.at[source_y], NEAR, rows - NEAR)):
                    number = y * 2 * X_HI * CORE + len(copies)
                    copies.append(pltpu.make_async_copy(source, held.at[shard, pl.ds(start, size), :], sems.at[number]))
        return copies

    def start_block(block):
        for y in range(block * per_block, (block + 1) * per_block):
            source_y = lax.rem(my_y - y + Y, Y)
            for kept in range(Y):

                @pl.when(source_y == kept)
                def _():
                    for copy in copies_of(y, kept, kept):
                        copy.start()

    def wait_block(block):
        for y in range(block * per_block, (block + 1) * per_block):
            for copy in copies_of(y, 0, 0):
                copy.wait()

    load_turns = pltpu.make_async_copy(turns_ref, turns, turns_sem)
    for load in loads:
        load.start()
    start_block(0)
    load_turns.start()
    for load in loads:
        load.wait()

    block_rows = BATCH * rows
    row = lax.broadcasted_iota(jnp.int32, (block_rows, HEAD_DIM), 0)
    is_first = lax.broadcasted_iota(jnp.int32, (block_rows, HEAD_DIM), 1) < HEAD_DIM // 2
    stores = []
    tail = None
    for first in range(0, shards, BATCH):
        if first + BATCH < shards:
            start_block(first // BATCH + 1)
        wait_block(first // BATCH)
        start = first * rows
        block = held[first : first + BATCH].reshape(block_rows, depth)
        projected = jnp.dot(block, w_flat[...], preferred_element_type=jnp.float32) + bias_ref[...]
        if start % SEQ_LEN == 0:
            tail = jnp.zeros((8, projected.shape[1]), jnp.float32)
        if first == 0:
            load_turns.wait()
        turn = turns[start : start + block_rows, :]
        other_turn = pltpu.roll(turn, HEAD_DIM // 2, 1)
        cosine = jnp.where(is_first, turn, other_turn)
        sine = jnp.where(is_first, -other_turn, turn)
        for head in range(heads):
            lanes = slice(head * HEAD_DIM, (head + 1) * HEAD_DIM)
            now = projected[:, lanes]
            before_one, before_two = tail[7:8, lanes], tail[6:7, lanes]
            previous_one = jnp.where(row == 0, before_one, pltpu.roll(now, 1, 0))
            previous_two = jnp.where(row == 0, before_two, jnp.where(row == 1, before_one, pltpu.roll(now, 2, 0)))
            part = taps_ref[0:1, lanes] * now + taps_ref[1:2, lanes] * previous_one + taps_ref[2:3, lanes] * previous_two
            turned = part * cosine + pltpu.roll(part, HEAD_DIM // 2, 1) * sine
            keys[head, start : start + block_rows, :] = turned.astype(keys.dtype)
        tail = projected[block_rows - 8 :]
        span = pl.ds(start, block_rows)
        stores.append(pltpu.make_async_copy(keys.at[:, span, :], out_ref.at[:, span, :], out_sems.at[first // BATCH]))
        stores[-1].start()
    for store in stores:
        store.wait()


def gate_kernel(*refs):
    del refs


def gated(value, *after):
    any_space = pl.BlockSpec(memory_space=pl.ANY)
    return pl.pallas_call(
        gate_kernel,
        in_specs=[any_space] * (1 + len(after)),
        out_specs=any_space,
        out_shape=jax.ShapeDtypeStruct(value.shape, value.dtype),
        input_output_aliases={0: 0},
        compiler_params=pltpu.CompilerParams(vmem_limit_bytes=2 * 1024 * 1024),
    )(value, *after)


def rotation(places):
    half_dim = HEAD_DIM // 2
    inv_freq = rope_base ** (-(jnp.arange(half_dim, dtype=jnp.float32) * 2.0) / HEAD_DIM)
    angles = places.astype(jnp.float32)[:, None] * inv_freq[None, :]
    return jnp.concatenate([jnp.cos(angles), jnp.sin(angles)], axis=1)


def keys_of(where, gathered, weight, bias, taps, turns):
    rows, depth = gathered[0].shape[1] + gathered[Y].shape[1], gathered[0].shape[2]
    shards = Y * X_HI * CORE
    columns = bias.shape[1]
    heads = columns // HEAD_DIM
    total = shards * rows
    vmem, any_space = pl.BlockSpec(memory_space=pltpu.VMEM), pl.BlockSpec(memory_space=pl.ANY)
    return pl.pallas_call(
        keys_kernel,
        in_specs=[pl.BlockSpec(memory_space=pltpu.SMEM)] + [any_space] * (len(gathered) + 1) + [vmem] * 2 + [any_space],
        out_specs=any_space,
        out_shape=jax.ShapeDtypeStruct((heads, total, HEAD_DIM), jnp.bfloat16),
        scratch_shapes=[
            pltpu.VMEM((shards, rows, depth), jnp.bfloat16),
            pltpu.VMEM((depth, columns), jnp.bfloat16),
            pltpu.VMEM((total, HEAD_DIM), jnp.float32),
            pltpu.VMEM((heads, total, HEAD_DIM), jnp.bfloat16),
            pltpu.SemaphoreType.DMA,
            pltpu.SemaphoreType.DMA((shards // BATCH,)),
            pltpu.SemaphoreType.DMA((weight.shape[0] * heads,)),
            pltpu.SemaphoreType.DMA((2 * shards,)),
        ],
        compiler_params=pltpu.CompilerParams(vmem_limit_bytes=56 * 1024 * 1024),
        cost_estimate=pl.CostEstimate(
            flops=2 * total * depth * columns,
            bytes_accessed=2 * (total * depth + depth * columns + total * columns),
            transcendentals=0,
        ),
    )(where, *gathered, weight, bias, taps, turns)


def along_y(value):
    def step(k):
        return lax.ppermute(value, "y", [(i, (i + k) % Y) for i in range(Y)])

    return [value] + [step(k) for k in range(1, Y)]


def body(fsdp, tensor, tokens, positions, key_weight, key_bias, conv_taps):
    rows, depth = tokens.shape
    piece, heads, _ = key_weight.shape
    columns = heads * HEAD_DIM

    own_weight = jnp.transpose(key_weight, (1, 0, 2))
    near_weight = lax.ppermute(own_weight, "x_lo", [(0, 1), (1, 0)])
    is_low = lax.axis_index("x_lo") == 0
    first = jnp.where(is_low, own_weight, near_weight)
    second = jnp.where(is_low, near_weight, own_weight)
    pair = jnp.concatenate([first, second], axis=1).reshape(heads * 2 * piece, HEAD_DIM)
    weight = lax.all_gather(pair, "z", axis=0)

    across = [(0, 1), (1, 0)]
    near, far = gated(tokens[:NEAR], pair), gated(tokens[NEAR:], pair)
    x_near = lax.ppermute(near, "x_hi", across)
    sent = jnp.broadcast_to(positions[None], (tensor, rows))
    places = lax.all_to_all(sent, ("y", "x_hi", "core"), 0, 0, tiled=True).reshape(-1)
    far_own = gated(jnp.stack(along_y(far)), x_near, places)
    far_other = lax.ppermute(far_own, "x_hi", across)
    near_all = along_y(gated(jnp.stack([near, x_near]), far_own))
    turns = rotation(gated(places, near_all[1]))
    near_all[2:] = [gated(piece, turns) for piece in near_all[2:]]
    gathered = (*near_all, far_own, far_other)
    gathered += tuple(lax.ppermute(piece, "core", across) for piece in gathered)
    where = jnp.stack([lax.axis_index("x_hi"), lax.axis_index("core"), lax.axis_index("y")])

    taps = jnp.transpose(conv_taps, (1, 0, 2)).reshape(conv_taps.shape[1], columns)
    bias = key_bias.astype(jnp.float32).reshape(1, columns)
    keys = keys_of(where, gathered, weight, bias, taps, turns)
    return jnp.transpose(keys, (1, 0, 2))


def solution(mesh):
    fsdp, tensor = mesh.shape["fsdp"], mesh.shape["tensor"]
    split = Mesh(mesh.devices.reshape(fsdp // 2, 2, Y, X_HI, CORE), ("z", "x_lo", "y", "x_hi", "core"))
    rows, heads = ("z", "x_lo"), ("y", "x_hi", "core")
    return jax.shard_map(
        lambda *args: body(fsdp, tensor, *args),
        mesh=split,
        in_specs=(P(rows + heads, None), P(rows + heads), P(rows, heads, None), P(heads, None), P(heads, None, None)),
        out_specs=P(rows, heads, None),
        check_vma=False,
    )
```

```python
import jax
import jax.numpy as jnp
from jax import lax
from jax.experimental import pallas as pl
from jax.experimental.pallas import tpu as pltpu
from jax.sharding import Mesh
from jax.sharding import PartitionSpec as P

HEAD_DIM = 128
SEQ_LEN = 1024
rope_base = 10000.0

Y, X_HI, CORE = 4, 2, 2
BATCH = 4
NEAR = 64


def keys_kernel(where_ref, *refs):
    count = Y + 2
    (*near_own, far_own_ref, far_other_ref), (*near_across, x_far_own_ref, x_far_other_ref) = refs[:count], refs[count : 2 * count]
    refs = refs[2 * count :]
    w_ref, bias_ref, taps_ref, turns_ref, out_ref, held, w_flat, turns, keys, turns_sem, out_sems, w_sems, sems = refs
    shards, rows, depth = held.shape
    pieces, heads = w_ref.shape[0], out_ref.shape[0]
    piece_rows = w_ref.shape[1] // heads
    my_x, my_core, my_y = where_ref[0], where_ref[1], where_ref[2]
    loads = []
    for piece in range(pieces):
        for head in range(heads):
            loads.append(
                pltpu.make_async_copy(
                    w_ref.at[piece, pl.ds(head * piece_rows, piece_rows), :],
                    w_flat.at[pl.ds(piece * piece_rows, piece_rows), pl.ds(head * HEAD_DIM, HEAD_DIM)],
                    w_sems.at[piece * heads + head],
                )
            )
    per_block = BATCH // (X_HI * CORE)

    def copies_of(y, source_y, kept):
        copies = []
        for x_step in range(X_HI):
            chip = y * X_HI + jnp.bitwise_xor(my_x, x_step)
            for core_step, near, far in (
                (0, near_own[kept], (far_own_ref, far_other_ref)[x_step]),
                (1, near_across[kept], (x_far_own_ref, x_far_other_ref)[x_step]),
            ):
                shard = chip * CORE + jnp.bitwise_xor(my_core, core_step)
                for source, start, size in ((near.at[x_step], 0, NEAR), (far.at[source_y], NEAR, rows - NEAR)):
                    number = y * 2 * X_HI * CORE + len(copies)
                    copies.append(pltpu.make_async_copy(source, held.at[shard, pl.ds(start, size), :], sems.at[number]))
        return copies

    def start_block(block):
        for y in range(block * per_block, (block + 1) * per_block):
            source_y = lax.rem(my_y - y + Y, Y)
            for kept in range(Y):

                @pl.when(source_y == kept)
                def _():
                    for copy in copies_of(y, kept, kept):
                        copy.start()

    def wait_block(block):
        for y in range(block * per_block, (block + 1) * per_block):
            for copy in copies_of(y, 0, 0):
                copy.wait()

    load_turns = pltpu.make_async_copy(turns_ref, turns, turns_sem)
    for load in loads:
        load.start()
    start_block(0)
    load_turns.start()
    for load in loads:
        load.wait()

    block_rows = BATCH * rows
    row = lax.broadcasted_iota(jnp.int32, (block_rows, HEAD_DIM), 0)
    is_first = lax.broadcasted_iota(jnp.int32, (block_rows, HEAD_DIM), 1) < HEAD_DIM // 2
    stores = []
    tail = None
    for first in range(0, shards, BATCH):
        if first + BATCH < shards:
            start_block(first // BATCH + 1)
        wait_block(first // BATCH)
        start = first * rows
        block = held[first : first + BATCH].reshape(block_rows, depth)
        projected = jnp.dot(block, w_flat[...], preferred_element_type=jnp.float32) + bias_ref[...]
        if start % SEQ_LEN == 0:
            tail = jnp.zeros((8, projected.shape[1]), jnp.float32)
        if first == 0:
            load_turns.wait()
        turn = turns[start : start + block_rows, :]
        other_turn = pltpu.roll(turn, HEAD_DIM // 2, 1)
        cosine = jnp.where(is_first, turn, other_turn)
        sine = jnp.where(is_first, -other_turn, turn)
        for head in range(heads):
            lanes = slice(head * HEAD_DIM, (head + 1) * HEAD_DIM)
            now = projected[:, lanes]
            before_one, before_two = tail[7:8, lanes], tail[6:7, lanes]
            previous_one = jnp.where(row == 0, before_one, pltpu.roll(now, 1, 0))
            previous_two = jnp.where(row == 0, before_two, jnp.where(row == 1, before_one, pltpu.roll(now, 2, 0)))
            part = taps_ref[0:1, lanes] * now + taps_ref[1:2, lanes] * previous_one + taps_ref[2:3, lanes] * previous_two
            turned = part * cosine + pltpu.roll(part, HEAD_DIM // 2, 1) * sine
            keys[head, start : start + block_rows, :] = turned.astype(keys.dtype)
        tail = projected[block_rows - 8 :]
        span = pl.ds(start, block_rows)
        stores.append(pltpu.make_async_copy(keys.at[:, span, :], out_ref.at[:, span, :], out_sems.at[first // BATCH]))
        stores[-1].start()
    for store in stores:
        store.wait()


def gate_kernel(*refs):
    del refs


def gated(value, *after):
    any_space = pl.BlockSpec(memory_space=pl.ANY)
    return pl.pallas_call(
        gate_kernel,
        in_specs=[any_space] * (1 + len(after)),
        out_specs=any_space,
        out_shape=jax.ShapeDtypeStruct(value.shape, value.dtype),
        input_output_aliases={0: 0},
        compiler_params=pltpu.CompilerParams(vmem_limit_bytes=2 * 1024 * 1024),
    )(value, *after)


def rotation(places):
    half_dim = HEAD_DIM // 2
    inv_freq = rope_base ** (-(jnp.arange(half_dim, dtype=jnp.float32) * 2.0) / HEAD_DIM)
    angles = places.astype(jnp.float32)[:, None] * inv_freq[None, :]
    return jnp.concatenate([jnp.cos(angles), jnp.sin(angles)], axis=1)


def keys_of(where, gathered, weight, bias, taps, turns):
    rows, depth = gathered[0].shape[1] + gathered[Y].shape[1], gathered[0].shape[2]
    shards = Y * X_HI * CORE
    columns = bias.shape[1]
    heads = columns // HEAD_DIM
    total = shards * rows
    vmem, any_space = pl.BlockSpec(memory_space=pltpu.VMEM), pl.BlockSpec(memory_space=pl.ANY)
    return pl.pallas_call(
        keys_kernel,
        in_specs=[pl.BlockSpec(memory_space=pltpu.SMEM)] + [any_space] * (len(gathered) + 1) + [vmem] * 2 + [any_space],
        out_specs=any_space,
        out_shape=jax.ShapeDtypeStruct((heads, total, HEAD_DIM), jnp.bfloat16),
        scratch_shapes=[
            pltpu.VMEM((shards, rows, depth), jnp.bfloat16),
            pltpu.VMEM((depth, columns), jnp.bfloat16),
            pltpu.VMEM((total, HEAD_DIM), jnp.float32),
            pltpu.VMEM((heads, total, HEAD_DIM), jnp.bfloat16),
            pltpu.SemaphoreType.DMA,
            pltpu.SemaphoreType.DMA((shards // BATCH,)),
            pltpu.SemaphoreType.DMA((weight.shape[0] * heads,)),
            pltpu.SemaphoreType.DMA((2 * shards,)),
        ],
        compiler_params=pltpu.CompilerParams(vmem_limit_bytes=56 * 1024 * 1024),
        cost_estimate=pl.CostEstimate(
            flops=2 * total * depth * columns,
            bytes_accessed=2 * (total * depth + depth * columns + total * columns),
            transcendentals=0,
        ),
    )(where, *gathered, weight, bias, taps, turns)


def along_y(value):
    def step(k):
        return lax.ppermute(value, "y", [(i, (i + k) % Y) for i in range(Y)])

    return [value] + [step(k) for k in range(1, Y)]


def body(fsdp, tensor, tokens, positions, key_weight, key_bias, conv_taps):
    rows, depth = tokens.shape
    piece, heads, _ = key_weight.shape
    columns = heads * HEAD_DIM

    own_weight = jnp.transpose(key_weight, (1, 0, 2))
    near_weight = lax.ppermute(own_weight, "x_lo", [(0, 1), (1, 0)])
    is_low = lax.axis_index("x_lo") == 0
    first = jnp.where(is_low, own_weight, near_weight)
    second = jnp.where(is_low, near_weight, own_weight)
    pair = jnp.concatenate([first, second], axis=1).reshape(heads * 2 * piece, HEAD_DIM)
    weight = lax.all_gather(pair, "z", axis=0)

    across = [(0, 1), (1, 0)]
    near, far = gated(tokens[:NEAR], pair), gated(tokens[NEAR:], pair)
    x_near = lax.ppermute(near, "x_hi", across)
    sent = jnp.broadcast_to(positions[None], (tensor, rows))
    places = lax.all_to_all(sent, ("y", "x_hi", "core"), 0, 0, tiled=True).reshape(-1)
    far_own = gated(jnp.stack(along_y(far)), x_near)
    far_other = lax.ppermute(far_own, "x_hi", across)
    where = jnp.stack([lax.axis_index("x_hi"), lax.axis_index("core"), lax.axis_index("y")])
    bias = key_bias.astype(jnp.float32).reshape(1, columns)
    near_all = along_y(gated(jnp.stack([near, x_near]), far_own, where, bias))
    turns = rotation(places)
    gathered = (*near_all, far_own, far_other)
    gathered += tuple(lax.ppermute(piece, "core", across) for piece in gathered)

    taps = jnp.transpose(conv_taps, (1, 0, 2)).reshape(conv_taps.shape[1], columns)
    keys = keys_of(where, gathered, weight, bias, taps, turns)
    return jnp.transpose(keys, (1, 0, 2))


def solution(mesh):
    fsdp, tensor = mesh.shape["fsdp"], mesh.shape["tensor"]
    split = Mesh(mesh.devices.reshape(fsdp // 2, 2, Y, X_HI, CORE), ("z", "x_lo", "y", "x_hi", "core"))
    rows, heads = ("z", "x_lo"), ("y", "x_hi", "core")
    return jax.shard_map(
        lambda *args: body(fsdp, tensor, *args),
        mesh=split,
        in_specs=(P(rows + heads, None), P(rows + heads), P(rows, heads, None), P(heads, None), P(heads, None, None)),
        out_specs=P(rows, heads, None),
        check_vma=False,
    )
```

```python
import jax
import jax.numpy as jnp
from jax import lax
from jax.experimental import pallas as pl
from jax.experimental.pallas import tpu as pltpu
from jax.sharding import Mesh
from jax.sharding import PartitionSpec as P

HEAD_DIM = 128
SEQ_LEN = 1024
rope_base = 10000.0

Y, X_HI, CORE = 4, 2, 2
BATCH = 4
NEAR = 64


def keys_kernel(where_ref, *refs):
    count = Y + 2
    (*near_own, far_own_ref, far_other_ref), (*near_across, x_far_own_ref, x_far_other_ref) = refs[:count], refs[count : 2 * count]
    refs = refs[2 * count :]
    w_ref, bias_ref, taps_ref, turns_ref, out_ref, held, w_flat, turns, keys, turns_sem, out_sems, w_sems, sems = refs
    shards, rows, depth = held.shape
    pieces, heads = w_ref.shape[0], out_ref.shape[0]
    piece_rows = w_ref.shape[1] // heads
    my_x, my_core, my_y = where_ref[0], where_ref[1], where_ref[2]
    loads = []
    for piece in range(pieces):
        for head in range(heads):
            loads.append(
                pltpu.make_async_copy(
                    w_ref.at[piece, pl.ds(head * piece_rows, piece_rows), :],
                    w_flat.at[pl.ds(piece * piece_rows, piece_rows), pl.ds(head * HEAD_DIM, HEAD_DIM)],
                    w_sems.at[piece * heads + head],
                )
            )
    per_block = BATCH // (X_HI * CORE)

    def copies_of(y, source_y, kept):
        copies = []
        for x_step in range(X_HI):
            chip = y * X_HI + jnp.bitwise_xor(my_x, x_step)
            for core_step, near, far in (
                (0, near_own[kept], (far_own_ref, far_other_ref)[x_step]),
                (1, near_across[kept], (x_far_own_ref, x_far_other_ref)[x_step]),
            ):
                shard = chip * CORE + jnp.bitwise_xor(my_core, core_step)
                for source, start, size in ((near.at[x_step], 0, NEAR), (far.at[source_y], NEAR, rows - NEAR)):
                    number = y * 2 * X_HI * CORE + len(copies)
                    copies.append(pltpu.make_async_copy(source, held.at[shard, pl.ds(start, size), :], sems.at[number]))
        return copies

    def start_block(block):
        for y in range(block * per_block, (block + 1) * per_block):
            source_y = lax.rem(my_y - y + Y, Y)
            for kept in range(Y):

                @pl.when(source_y == kept)
                def _():
                    for copy in copies_of(y, kept, kept):
                        copy.start()

    def wait_block(block):
        for y in range(block * per_block, (block + 1) * per_block):
            for copy in copies_of(y, 0, 0):
                copy.wait()

    load_turns = pltpu.make_async_copy(turns_ref, turns, turns_sem)
    for load in loads:
        load.start()
    start_block(0)
    load_turns.start()
    for load in loads:
        load.wait()

    block_rows = BATCH * rows
    row = lax.broadcasted_iota(jnp.int32, (block_rows, HEAD_DIM), 0)
    is_first = lax.broadcasted_iota(jnp.int32, (block_rows, HEAD_DIM), 1) < HEAD_DIM // 2
    stores = []
    tail = None
    for first in range(0, shards, BATCH):
        if first + BATCH < shards:
            start_block(first // BATCH + 1)
        wait_block(first // BATCH)
        start = first * rows
        block = held[first : first + BATCH].reshape(block_rows, depth)
        projected = jnp.dot(block, w_flat[...], preferred_element_type=jnp.float32) + bias_ref[...]
        if start % SEQ_LEN == 0:
            tail = jnp.zeros((8, projected.shape[1]), jnp.float32)
        if first == 0:
            load_turns.wait()
        turn = turns[start : start + block_rows, :]
        other_turn = pltpu.roll(turn, HEAD_DIM // 2, 1)
        cosine = jnp.where(is_first, turn, other_turn)
        sine = jnp.where(is_first, -other_turn, turn)
        for head in range(heads):
            lanes = slice(head * HEAD_DIM, (head + 1) * HEAD_DIM)
            now = projected[:, lanes]
            before_one, before_two = tail[7:8, lanes], tail[6:7, lanes]
            previous_one = jnp.where(row == 0, before_one, pltpu.roll(now, 1, 0))
            previous_two = jnp.where(row == 0, before_two, jnp.where(row == 1, before_one, pltpu.roll(now, 2, 0)))
            part = taps_ref[0:1, lanes] * now + taps_ref[1:2, lanes] * previous_one + taps_ref[2:3, lanes] * previous_two
            turned = part * cosine + pltpu.roll(part, HEAD_DIM // 2, 1) * sine
            keys[head, start : start + block_rows, :] = turned.astype(keys.dtype)
        tail = projected[block_rows - 8 :]
        span = pl.ds(start, block_rows)
        stores.append(pltpu.make_async_copy(keys.at[:, span, :], out_ref.at[:, span, :], out_sems.at[first // BATCH]))
        stores[-1].start()
    for store in stores:
        store.wait()


def gate_kernel(*refs):
    del refs


def gated(value, *after):
    any_space = pl.BlockSpec(memory_space=pl.ANY)
    return pl.pallas_call(
        gate_kernel,
        in_specs=[any_space] * (1 + len(after)),
        out_specs=any_space,
        out_shape=jax.ShapeDtypeStruct(value.shape, value.dtype),
        input_output_aliases={0: 0},
        compiler_params=pltpu.CompilerParams(vmem_limit_bytes=2 * 1024 * 1024),
    )(value, *after)


def rotation(places):
    half_dim = HEAD_DIM // 2
    inv_freq = rope_base ** (-(jnp.arange(half_dim, dtype=jnp.float32) * 2.0) / HEAD_DIM)
    angles = places.astype(jnp.float32)[:, None] * inv_freq[None, :]
    return jnp.concatenate([jnp.cos(angles), jnp.sin(angles)], axis=1)


def keys_of(where, gathered, weight, bias, taps, turns):
    rows, depth = gathered[0].shape[1] + gathered[Y].shape[1], gathered[0].shape[2]
    shards = Y * X_HI * CORE
    columns = bias.shape[1]
    heads = columns // HEAD_DIM
    total = shards * rows
    vmem, any_space = pl.BlockSpec(memory_space=pltpu.VMEM), pl.BlockSpec(memory_space=pl.ANY)
    return pl.pallas_call(
        keys_kernel,
        in_specs=[pl.BlockSpec(memory_space=pltpu.SMEM)] + [any_space] * (len(gathered) + 1) + [vmem] * 2 + [any_space],
        out_specs=any_space,
        out_shape=jax.ShapeDtypeStruct((heads, total, HEAD_DIM), jnp.bfloat16),
        scratch_shapes=[
            pltpu.VMEM((shards, rows, depth), jnp.bfloat16),
            pltpu.VMEM((depth, columns), jnp.bfloat16),
            pltpu.VMEM((total, HEAD_DIM), jnp.float32),
            pltpu.VMEM((heads, total, HEAD_DIM), jnp.bfloat16),
            pltpu.SemaphoreType.DMA,
            pltpu.SemaphoreType.DMA((shards // BATCH,)),
            pltpu.SemaphoreType.DMA((weight.shape[0] * heads,)),
            pltpu.SemaphoreType.DMA((2 * shards,)),
        ],
        compiler_params=pltpu.CompilerParams(vmem_limit_bytes=56 * 1024 * 1024),
        cost_estimate=pl.CostEstimate(
            flops=2 * total * depth * columns,
            bytes_accessed=2 * (total * depth + depth * columns + total * columns),
            transcendentals=0,
        ),
    )(where, *gathered, weight, bias, taps, turns)


def along_y(value):
    def step(k):
        return lax.ppermute(value, "y", [(i, (i + k) % Y) for i in range(Y)])

    return [value] + [step(k) for k in range(1, Y)]


def body(fsdp, tensor, tokens, positions, key_weight, key_bias, conv_taps):
    rows, depth = tokens.shape
    piece, heads, _ = key_weight.shape
    columns = heads * HEAD_DIM

    own_weight = jnp.transpose(key_weight, (1, 0, 2))
    near_weight = lax.ppermute(own_weight, "x_lo", [(0, 1), (1, 0)])
    is_low = lax.axis_index("x_lo") == 0
    first = jnp.where(is_low, own_weight, near_weight)
    second = jnp.where(is_low, near_weight, own_weight)
    pair = jnp.concatenate([first, second], axis=1).reshape(heads * 2 * piece, HEAD_DIM)
    weight = lax.all_gather(pair, "z", axis=0)

    across = [(0, 1), (1, 0)]
    near, far = gated(tokens[:NEAR], pair), gated(tokens[NEAR:], pair)
    x_near = lax.ppermute(near, "x_hi", across)
    far_own = gated(jnp.stack(along_y(far)), x_near)
    far_other = lax.ppermute(far_own, "x_hi", across)
    where = jnp.stack([lax.axis_index("x_hi"), lax.axis_index("core"), lax.axis_index("y")])
    bias = key_bias.astype(jnp.float32).reshape(1, columns)
    near_all = along_y(gated(jnp.stack([near, x_near]), far_own, where, bias))
    x_first = lax.ppermute(near_all[0], "core", across)
    sent = gated(jnp.broadcast_to(positions[None], (tensor, rows)), x_first)
    places = lax.all_to_all(sent, ("y", "x_hi", "core"), 0, 0, tiled=True).reshape(-1)
    turns = rotation(places)
    far_other = gated(far_other, places)
    gathered = (*near_all, far_own, far_other)
    gathered += (x_first, *(lax.ppermute(piece, "core", across) for piece in gathered[1:]))

    taps = jnp.transpose(conv_taps, (1, 0, 2)).reshape(conv_taps.shape[1], columns)
    keys = keys_of(where, gathered, weight, bias, taps, turns)
    return jnp.transpose(keys, (1, 0, 2))


def solution(mesh):
    fsdp, tensor = mesh.shape["fsdp"], mesh.shape["tensor"]
    split = Mesh(mesh.devices.reshape(fsdp // 2, 2, Y, X_HI, CORE), ("z", "x_lo", "y", "x_hi", "core"))
    rows, heads = ("z", "x_lo"), ("y", "x_hi", "core")
    return jax.shard_map(
        lambda *args: body(fsdp, tensor, *args),
        mesh=split,
        in_specs=(P(rows + heads, None), P(rows + heads), P(rows, heads, None), P(heads, None), P(heads, None, None)),
        out_specs=P(rows, heads, None),
        check_vma=False,
    )
```

```python
import jax
import jax.numpy as jnp
from jax import lax
from jax.experimental import pallas as pl
from jax.experimental.pallas import tpu as pltpu
from jax.sharding import Mesh
from jax.sharding import PartitionSpec as P

HEAD_DIM = 128
SEQ_LEN = 1024
rope_base = 10000.0

Y, X_HI, CORE = 4, 2, 2
BATCH = 4
NEAR = 64


def keys_kernel(where_ref, *refs):
    count = Y + 2
    (*near_own, far_own_ref, far_other_ref), (*near_across, x_far_own_ref, x_far_other_ref) = refs[:count], refs[count : 2 * count]
    refs = refs[2 * count :]
    w_ref, bias_ref, taps_ref, cos_ref, sin_ref, out_ref, held, w_flat, keys, out_sems, w_sems, sems = refs
    shards, rows, depth = held.shape
    pieces, heads = w_ref.shape[0], out_ref.shape[0]
    piece_rows = w_ref.shape[1] // heads
    my_x, my_core, my_y = where_ref[0], where_ref[1], where_ref[2]
    loads = []
    for piece in range(pieces):
        for head in range(heads):
            loads.append(
                pltpu.make_async_copy(
                    w_ref.at[piece, pl.ds(head * piece_rows, piece_rows), :],
                    w_flat.at[pl.ds(piece * piece_rows, piece_rows), pl.ds(head * HEAD_DIM, HEAD_DIM)],
                    w_sems.at[piece * heads + head],
                )
            )
    per_block = BATCH // (X_HI * CORE)

    def copies_of(y, source_y, kept):
        copies = []
        for x_step in range(X_HI):
            chip = y * X_HI + jnp.bitwise_xor(my_x, x_step)
            for core_step, near, far in (
                (0, near_own[kept], (far_own_ref, far_other_ref)[x_step]),
                (1, near_across[kept], (x_far_own_ref, x_far_other_ref)[x_step]),
            ):
                shard = chip * CORE + jnp.bitwise_xor(my_core, core_step)
                for source, start, size in ((near.at[x_step], 0, NEAR), (far.at[source_y], NEAR, rows - NEAR)):
                    number = y * 2 * X_HI * CORE + len(copies)
                    copies.append(pltpu.make_async_copy(source, held.at[shard, pl.ds(start, size), :], sems.at[number]))
        return copies

    def start_block(block):
        for y in range(block * per_block, (block + 1) * per_block):
            source_y = lax.rem(my_y - y + Y, Y)
            for kept in range(Y):

                @pl.when(source_y == kept)
                def _():
                    for copy in copies_of(y, kept, kept):
                        copy.start()

    def wait_block(block):
        for y in range(block * per_block, (block + 1) * per_block):
            for copy in copies_of(y, 0, 0):
                copy.wait()

    for load in loads:
        load.start()
    start_block(0)
    for load in loads:
        load.wait()

    block_rows = BATCH * rows
    row = lax.broadcasted_iota(jnp.int32, (block_rows, HEAD_DIM), 0)
    stores = []
    tail = None
    for first in range(0, shards, BATCH):
        if first + BATCH < shards:
            start_block(first // BATCH + 1)
        wait_block(first // BATCH)
        start = first * rows
        block = held[first : first + BATCH].reshape(block_rows, depth)
        projected = jnp.dot(block, w_flat[...], preferred_element_type=jnp.float32) + bias_ref[...]
        if start % SEQ_LEN == 0:
            tail = jnp.zeros((8, projected.shape[1]), jnp.float32)
        half_cosine = cos_ref[start : start + block_rows, :]
        half_sine = sin_ref[start : start + block_rows, :]
        cosine = jnp.concatenate([half_cosine, half_cosine], axis=1)
        sine = jnp.concatenate([-half_sine, half_sine], axis=1)
        for head in range(heads):
            lanes = slice(head * HEAD_DIM, (head + 1) * HEAD_DIM)
            now = projected[:, lanes]
            before_one, before_two = tail[7:8, lanes], tail[6:7, lanes]
            previous_one = jnp.where(row == 0, before_one, pltpu.roll(now, 1, 0))
            previous_two = jnp.where(row == 0, before_two, jnp.where(row == 1, before_one, pltpu.roll(now, 2, 0)))
            part = taps_ref[0:1, lanes] * now + taps_ref[1:2, lanes] * previous_one + taps_ref[2:3, lanes] * previous_two
            turned = part * cosine + pltpu.roll(part, HEAD_DIM // 2, 1) * sine
            keys[head, start : start + block_rows, :] = turned.astype(keys.dtype)
        tail = projected[block_rows - 8 :]
        span = pl.ds(start, block_rows)
        stores.append(pltpu.make_async_copy(keys.at[:, span, :], out_ref.at[:, span, :], out_sems.at[first // BATCH]))
        stores[-1].start()
    for store in stores:
        store.wait()


def gate_kernel(*refs):
    del refs


def gated(value, *after):
    any_space = pl.BlockSpec(memory_space=pl.ANY)
    return pl.pallas_call(
        gate_kernel,
        in_specs=[any_space] * (1 + len(after)),
        out_specs=any_space,
        out_shape=jax.ShapeDtypeStruct(value.shape, value.dtype),
        input_output_aliases={0: 0},
        compiler_params=pltpu.CompilerParams(vmem_limit_bytes=2 * 1024 * 1024),
    )(value, *after)


def rotation(places):
    half_dim = HEAD_DIM // 2
    inv_freq = rope_base ** (-(jnp.arange(half_dim, dtype=jnp.float32) * 2.0) / HEAD_DIM)
    angles = places.astype(jnp.float32)[:, None] * inv_freq[None, :]
    return jnp.cos(angles), jnp.sin(angles)


def keys_of(where, gathered, weight, bias, taps, *turns):
    rows, depth = gathered[0].shape[1] + gathered[Y].shape[1], gathered[0].shape[2]
    shards = Y * X_HI * CORE
    columns = bias.shape[1]
    heads = columns // HEAD_DIM
    total = shards * rows
    vmem, any_space = pl.BlockSpec(memory_space=pltpu.VMEM), pl.BlockSpec(memory_space=pl.ANY)
    return pl.pallas_call(
        keys_kernel,
        in_specs=[pl.BlockSpec(memory_space=pltpu.SMEM)] + [any_space] * (len(gathered) + 1) + [vmem] * 4,
        out_specs=any_space,
        out_shape=jax.ShapeDtypeStruct((heads, total, HEAD_DIM), jnp.bfloat16),
        scratch_shapes=[
            pltpu.VMEM((shards, rows, depth), jnp.bfloat16),
            pltpu.VMEM((depth, columns), jnp.bfloat16),
            pltpu.VMEM((heads, total, HEAD_DIM), jnp.bfloat16),
            pltpu.SemaphoreType.DMA((shards // BATCH,)),
            pltpu.SemaphoreType.DMA((weight.shape[0] * heads,)),
            pltpu.SemaphoreType.DMA((2 * shards,)),
        ],
        compiler_params=pltpu.CompilerParams(vmem_limit_bytes=56 * 1024 * 1024),
        cost_estimate=pl.CostEstimate(
            flops=2 * total * depth * columns,
            bytes_accessed=2 * (total * depth + depth * columns + total * columns),
            transcendentals=0,
        ),
    )(where, *gathered, weight, bias, taps, *turns)


def along_y(value):
    def step(k):
        return lax.ppermute(value, "y", [(i, (i + k) % Y) for i in range(Y)])

    return [value] + [step(k) for k in range(1, Y)]


def body(fsdp, tensor, tokens, positions, key_weight, key_bias, conv_taps):
    rows, depth = tokens.shape
    piece, heads, _ = key_weight.shape
    columns = heads * HEAD_DIM

    own_weight = jnp.transpose(key_weight, (1, 0, 2))
    near_weight = lax.ppermute(own_weight, "x_lo", [(0, 1), (1, 0)])
    is_low = lax.axis_index("x_lo") == 0
    first = jnp.where(is_low, own_weight, near_weight)
    second = jnp.where(is_low, near_weight, own_weight)
    pair = jnp.concatenate([first, second], axis=1).reshape(heads * 2 * piece, HEAD_DIM)
    weight = lax.all_gather(pair, "z", axis=0)

    across = [(0, 1), (1, 0)]
    near, far = gated(tokens[:NEAR], pair), gated(tokens[NEAR:], pair)
    x_near = lax.ppermute(near, "x_hi", across)
    sent = jnp.broadcast_to(positions[None], (tensor, rows))
    places = lax.all_to_all(sent, ("y", "x_hi", "core"), 0, 0, tiled=True).reshape(-1)
    far_own = gated(jnp.stack(along_y(far)), x_near)
    far_other = lax.ppermute(far_own, "x_hi", across)
    where = jnp.stack([lax.axis_index("x_hi"), lax.axis_index("core"), lax.axis_index("y")])
    bias = key_bias.astype(jnp.float32).reshape(1, columns)
    near_all = along_y(gated(jnp.stack([near, x_near]), far_own, where, bias))
    turns = rotation(places)
    gathered = (*near_all, far_own, far_other)
    gathered += tuple(lax.ppermute(piece, "core", across) for piece in gathered)

    taps = jnp.transpose(conv_taps, (1, 0, 2)).reshape(conv_taps.shape[1], columns)
    keys = keys_of(where, gathered, weight, bias, taps, *turns)
    return jnp.transpose(keys, (1, 0, 2))


def solution(mesh):
    fsdp, tensor = mesh.shape["fsdp"], mesh.shape["tensor"]
    split = Mesh(mesh.devices.reshape(fsdp // 2, 2, Y, X_HI, CORE), ("z", "x_lo", "y", "x_hi", "core"))
    rows, heads = ("z", "x_lo"), ("y", "x_hi", "core")
    return jax.shard_map(
        lambda *args: body(fsdp, tensor, *args),
        mesh=split,
        in_specs=(P(rows + heads, None), P(rows + heads), P(rows, heads, None), P(heads, None), P(heads, None, None)),
        out_specs=P(rows, heads, None),
        check_vma=False,
    )
```
